32 devices in a mesh: groups: 2 (over y), gx: 16 (over z, x, core).
Axes of the slice: x: 2, y: 2, z: 4, core: 2. Of those that a mesh axis runs over, the one named last changes fastest.
Arguments:
- activations: bfloat16 [128, 16, 16, 512], P(('groups', 'gx')), parts along dimension 0, may hold values from -6 to 6
- first_kernel: bfloat16 [3, 3, 3, 16, 32], replicated, may hold values from -0.3125 to 0.3125
- second_kernel: bfloat16 [3, 3, 3, 32, 64], replicated, may hold values from -0.21875 to 0.21875
- head_weight: float32 [64], replicated, may hold values from -1.5 to 1.5
- labels: int32 [32, 4, 128], P(('groups', 'gx')), parts along dimension 0, may hold values 0 or 1
Outputs:
- input_grad: bfloat16 [128, 16, 16, 512], P(('groups', 'gx')), parts along dimension 0
- first_grad: float32 [6, 3, 3, 16, 32], P('groups'), parts along dimension 0
- second_grad: float32 [6, 3, 3, 32, 64], P('groups'), parts along dimension 0
- head_grad: float32 [128], P('groups'), parts along dimension 0
The draws below stay inside these ranges and needn't reach their ends.
There are 2 independent parts, one for each index of `groups`. The reference program is written for one: setup_inputs(seed, part) draws one part's arguments, and reference() takes and returns one part's arrays. A program takes and returns all parts, laid end to end along the dimension named above; an argument that names none is the same for every part. Nothing has to cross between parts.
All inputs are finite; a program needn't handle non-finite values. No bound on the sum of `labels` on one device may be relied on, other than what follows from the above.
Results may differ from the reference program's by a relative error of at most 0.0062.
Values may be sent and summed in bfloat16 or wider, within the bound.
A program may use at most 128 MiB of HBM per device.

```python
import jax
import jax.numpy as jnp
from jax import lax

C0 = 16
C1 = 32
C2 = 64
Y = 16
Z = 512
X = 64


def set_ends(entries, key, smallest, top_value):
    spot = [jax.random.randint(jax.random.fold_in(key, axis), (), 0, length) for axis, length in enumerate(entries.shape)]
    main_axis = entries.shape.index(max(entries.shape))
    next_to = spot[:main_axis] + [(spot[main_axis] + 1) % entries.shape[main_axis]] + spot[main_axis + 1:]
    return entries.at[tuple(spot)].set(smallest).at[tuple(next_to)].set(top_value)


def steps_of(own_key, dims, shards, low, top_value):
    loudness = 1.0
    for position, parts in shards:
        steps = jax.random.uniform(jax.random.fold_in(jax.random.fold_in(own_key, 6), position), (parts,), jnp.float32, low / len(shards), top_value / len(shards))
        loudness = loudness * jnp.repeat(jnp.exp(steps), dims[position] // parts).reshape((-1,) + (1,) * (len(dims) - 1 - position))
    return loudness


def bell_draw(rng, dims, deviation, limit, pieces=(), dtype=jnp.bfloat16):
    level = steps_of(rng, dims, pieces, -0.22, 0.18) if pieces else 1.0
    entries = jax.random.normal(rng, dims, jnp.float32) * deviation * level
    return jnp.minimum(jnp.maximum(entries, -limit), limit).astype(dtype)


def setup_inputs(seed: int = 0, part: int = 0) -> dict:
    keys = jax.random.split(jax.random.key(seed), 6)
    part_splits = jax.random.split(jax.random.fold_in(keys[5], part), 6)
    activations = bell_draw(part_splits[0], (X, Y, C0, Z), 1.0, 6.0, ((0, 16),))
    first_kernel = bell_draw(keys[1], (3, 3, 3, C0, C1), (27 * C0) ** -0.5, 0.3125)
    second_kernel = bell_draw(keys[2], (3, 3, 3, C1, C2), (27 * C1) ** -0.5, 0.21875)
    head_weight = bell_draw(keys[3], (C2,), 16 ** -0.5, 1.5, (), jnp.float32)
    labels = set_ends((jax.random.randint(part_splits[4], (X // 4, Y // 4, Z // 4), 0, 10) < 3).astype(jnp.int32), jax.random.fold_in(part_splits[4], 1), 0, 1)
    return {"activations": activations, "first_kernel": first_kernel, "second_kernel": second_kernel, "head_weight": head_weight, "labels": labels}


FORWARD_SPEC = ('NXYCZ', 'XYZIO', 'NXYCZ')
BACKWARD_SPEC = ('NXYCZ', 'XYZOI', 'NXYCZ')

def forward_conv(volume, kernel, x_padding):
    return lax.conv_general_dilated(volume[None], kernel, (2, 2, 2), (x_padding, (1, 1), (1, 1)), dimension_numbers=FORWARD_SPEC, preferred_element_type=jnp.float32)[0]

def input_grad_conv(slope, kernel, x_padding):
    flipped = kernel[::-1, ::-1, ::-1]
    return lax.conv_general_dilated(slope[None], flipped, (1, 1, 1), (x_padding, (1, 2), (1, 2)), lhs_dilation=(2, 2, 2), dimension_numbers=BACKWARD_SPEC, preferred_element_type=jnp.float32)[0]

def weight_grad(padded, slope):
    out_x, out_y, out_c, out_z = slope.shape
    slope_wide = slope.astype(jnp.float32)
    blocks = []
    for offset_x in range(3):
        for offset_y in range(3):
            for offset_z in range(3):
                strided = lax.slice(padded, (offset_x, offset_y, 0, offset_z), (offset_x + 2 * out_x - 1, offset_y + 2 * out_y - 1, padded.shape[2], offset_z + 2 * out_z - 1), (2, 2, 1, 2))
                blocks.append(jnp.einsum('xycz,xydz->cd', strided.astype(jnp.float32), slope_wide))
    return jnp.stack(blocks).reshape(3, 3, 3, padded.shape[2], out_c)

def silu_slope(value):
    sig = jax.nn.sigmoid(value)
    return sig * (1.0 + value * (1.0 - sig))

def reference(activations, first_kernel, second_kernel, head_weight, labels):
    pre_first = forward_conv(activations, first_kernel, (1, 1))
    act_first = jax.nn.silu(pre_first).astype(jnp.bfloat16)
    pre_second = forward_conv(act_first, second_kernel, (1, 1))
    act_second = jax.nn.silu(pre_second)
    logits = lax.optimization_barrier(jnp.sum(act_second * head_weight[None, None, :, None], axis=2))
    logit_grad = jax.nn.sigmoid(logits) - labels.astype(jnp.float32)
    inverse_count = 1.0 / labels.size
    head_grad = lax.optimization_barrier(jnp.sum(logit_grad[:, :, None, :] * act_second, axis=(0, 1, 3))) * inverse_count
    second_slope = (logit_grad[:, :, None, :] * head_weight[None, None, :, None] * silu_slope(pre_second)).astype(jnp.bfloat16)
    padded_mid = jnp.pad(act_first, ((1, 1), (1, 1), (0, 0), (1, 1)))
    second_grad = weight_grad(padded_mid, second_slope) * inverse_count
    first_back = input_grad_conv(second_slope, second_kernel, (1, 2))
    first_slope = (first_back * silu_slope(pre_first)).astype(jnp.bfloat16)
    padded_in = jnp.pad(activations, ((1, 1), (1, 1), (0, 0), (1, 1)))
    first_grad = weight_grad(padded_in, first_slope) * inverse_count
    input_grad = input_grad_conv(first_slope, first_kernel, (1, 2)).astype(jnp.bfloat16)
    return (input_grad, first_grad, second_grad, head_grad)
```

```python
import functools

import jax
import jax.numpy as jnp
from jax import lax
from jax.experimental import pallas as pl
from jax.experimental.pallas import tpu as pltpu
from jax.sharding import PartitionSpec as P

F32 = jnp.float32
BF16 = jnp.bfloat16
MESH = pl.DeviceIdType.MESH


def mm(left, right):
    return lax.dot_general(left, right, (((1,), (0,)), ((), ())), preferred_element_type=F32)


def mm_nt(left, right):
    return lax.dot_general(left, right, (((1,), (1,)), ((), ())), preferred_element_type=F32)


def iota(shape, axis):
    return lax.broadcasted_iota(jnp.int32, shape, axis)


def one_hot(condition):
    return jnp.where(condition, 1.0, 0.0).astype(BF16)


def each(count, body):
    def step(index, carry):
        body(index)
        return carry

    lax.fori_loop(0, count, step, 0, unroll=True)


def rows(start, size, align=16):
    return pl.ds(pl.multiple_of(start, align), size)


def roll_masked(value, shift, empty_lane):
    rolled = pltpu.roll(value, shift, axis=1)
    return jnp.where(iota(value.shape, 1) == empty_lane, 0.0, rolled)


def kernel(
    n, p1, p2, inverse_count,
    act, w1, w2, hw, labels,
    out, fg_out, sg_out, head_out,
    A, B, S2, SU, F2, slope1, IGp, spread, gather, w1t, w2t, bd1, bd2,
    abuf, sbuf, fbuf, halo_a, halo_b, halo_s, halo_f,
    G1, R1, T1, G2, R2, T2,
    halo_send, halo_recv, rs1_s, rs1_r, ag1_s, ag1_r, rs2_s, rs2_r, ag2_s, ag2_r,
):
    me = lax.axis_index("gx")
    group = lax.axis_index("groups")
    has_lower = me > 0
    has_upper = me < n - 1

    def partner(d):
        return lax.rem(me + d, n)

    barrier = pltpu.get_barrier_semaphore()

    def greet(d, carry):
        pl.semaphore_signal(barrier, inc=1, device_id=(group, partner(d)), device_id_type=MESH)
        return carry

    lax.fori_loop(1, n, greet, 0)

    z_row = iota((512, 640), 0)
    lane = iota((512, 640), 1)
    spread[...] = one_hot(z_row == 4 * (lane & 127) + (lane >> 7) - 1)
    src = iota((512, 512), 0)
    gather[...] = one_hot(iota((512, 512), 1) == 4 * (src & 127) + 2 * ((src >> 7) & 1) + (src >> 8))

    pl.semaphore_wait(barrier, n - 1)

    def halo(slot, source, target, to):
        return pltpu.make_async_remote_copy(
            src_ref=source, dst_ref=target, send_sem=halo_send.at[slot], recv_sem=halo_recv.at[slot],
            device_id=(group, to), device_id_type=MESH,
        )

    up = lax.rem(me + 1, n)
    down = lax.rem(me + n - 1, n)
    send_a = halo(0, act.at[3], halo_a, up)
    send_b = halo(1, abuf, halo_b, up)
    send_s = halo(2, sbuf, halo_s, down)
    send_f = halo(3, fbuf, halo_f, down)

    @pl.when(has_upper)
    def _():
        send_a.start()

    eye32 = one_hot(iota((32, 32), 0) == iota((32, 32), 1))
    eye64 = one_hot(iota((64, 64), 0) == iota((64, 64), 1))
    for a in range(3):
        w1t[a] = mm_nt(eye32, w1[a * 144:(a + 1) * 144, :]).astype(BF16)
        w2t[a] = mm_nt(eye64, w2[a * 288:(a + 1) * 288, :]).astype(BF16)
    for place, a in enumerate((1, 2, 0)):
        def k1(b, c):
            at = (a * 9 + b * 3 + c) * 16
            return w1[at:at + 16, :].astype(F32)

        def k2(b, c):
            at = (a * 9 + b * 3 + c) * 32
            return w2[at:at + 32, :].astype(F32)

        zero1 = jnp.zeros((16, 32), F32)
        zero2 = jnp.zeros((32, 64), F32)
        for k, zero, dest, height in ((k1, zero1, bd1, 16), (k2, zero2, bd2, 32)):
            table = (
                (k(1, 1), zero, zero, zero),
                (k(1, 2), k(1, 0), zero, zero),
                (k(2, 1), zero, k(0, 1), zero),
                (k(2, 2), k(2, 0), k(0, 2), k(0, 0)),
            )
            for q, parts in enumerate(table):
                at = place * 4 * height + q * height
                dest[at:at + height, :] = jnp.concatenate(parts, axis=1).astype(BF16)

    for x in range(5):
        A[x, 0:48, :] = jnp.zeros((48, 256), BF16)
    for x in range(3):
        B[x, 0:96, :] = jnp.zeros((96, 128), BF16)
        F2[x, 512:576, :] = jnp.zeros((64, 256), BF16)
    S2[512:640, :] = jnp.zeros((128, 128), BF16)
    SU[512:640, :] = jnp.zeros((128, 128), BF16)

    def fill_a(x, plane):
        phases = mm(plane, spread[...]).astype(BF16)
        for y in range(16):
            part = phases[y * 16:(y + 1) * 16, :]
            for c in range(3):
                at = (y + 1) * 48 + c * 16
                A[x, at:at + 16, 0:128] = part[:, c * 128:(c + 1) * 128]
                A[x, at:at + 16, 128:256] = part[:, (c + 2) * 128:(c + 3) * 128]

    def fill_b(x, j, value):
        even = value[:, 0:128]
        odd = value[:, 128:256]
        back = roll_masked(odd.astype(F32), 1, 0).astype(BF16)
        at = (j + 1) * 96
        B[x, rows(at, 32), :] = back
        B[x, rows(at + 32, 32), :] = even
        B[x, rows(at + 64, 32), :] = odd

    def first_section(i):
        def body(j):
            at = rows(j * 96, 144)
            pre = mm(w1t[0], A[2 * i, at, :]) + mm(w1t[1], A[2 * i + 1, at, :]) + mm(w1t[2], A[2 * i + 2, at, :])
            sig = jax.nn.sigmoid(pre)
            slope1[i, rows(j * 32, 32), :] = sig * (1.0 + pre * (1.0 - sig))
            value = (pre * sig).astype(BF16)
            if i == 1:
                abuf[rows(j * 32, 32), :] = value
            fill_b(i + 1, j, value)

        each(8, body)

    for x in (1, 2, 3):
        fill_a(x + 1, act[x])
    first_section(1)

    @pl.when(has_upper)
    def _():
        send_b.start()

    fill_a(1, act[0])

    @pl.when(has_lower)
    def _():
        send_a.wait_recv()
        fill_a(0, halo_a[...])

    @pl.when(jnp.logical_not(has_lower))
    def _():
        A[0] = jnp.zeros((816, 256), BF16)

    first_section(0)

    @pl.when(has_lower)
    def _():
        send_b.wait_recv()
        each(8, lambda j: fill_b(0, j, halo_b[rows(j * 32, 32), :]))

    @pl.when(jnp.logical_not(has_lower))
    def _():
        B[0] = jnp.zeros((864, 128), BF16)

    diagonal = iota((64, 64), 0) == iota((64, 64), 1)
    weight = jnp.sum(jnp.where(diagonal, hw[...], 0.0), axis=1, keepdims=True)

    def fill_s(target, j, value):
        at = j * 128
        target[rows(at, 64), :] = value
        target[rows(at + 64, 64), :] = roll_masked(value.astype(F32), 127, 127).astype(BF16)

    head = jnp.zeros((64, 128), F32)
    for j in range(4):
        at = slice(j * 192, j * 192 + 288)
        pre = mm(w2t[0], B[0, at, :]) + mm(w2t[1], B[1, at, :]) + mm(w2t[2], B[2, at, :])
        sig = jax.nn.sigmoid(pre)
        act2 = pre * sig
        logits = jnp.sum(act2 * weight, axis=0, keepdims=True)
        logit_grad = jax.nn.sigmoid(logits) - labels[0, j:j + 1, :].astype(F32)
        head = head + logit_grad * act2
        slope = (logit_grad * weight * (sig * (1.0 + pre * (1.0 - sig)))).astype(BF16)
        sbuf[j * 64:(j + 1) * 64, :] = slope
        fill_s(S2, j, slope)
    head = jnp.sum(head, axis=1, keepdims=True) * inverse_count

    @pl.when(has_lower)
    def _():
        send_s.start()

    def fill_f(plane, j, value):
        even = value[:, 0:128]
        ahead = roll_masked(even.astype(F32), 127, 127).astype(BF16)
        at = j * 64
        F2[plane, rows(at, 32), :] = value
        F2[plane, rows(at + 32, 32), 0:128] = value[:, 128:256]
        F2[plane, rows(at + 32, 32), 128:256] = ahead

    def first_back(plane, j, back):
        for q in range(2):
            at = (2 * j + q) * 32
            both = jnp.concatenate((back[q * 64:q * 64 + 32, :], back[q * 64 + 32:q * 64 + 64, :]), axis=1)
            value = (both * slope1[plane, rows(at, 32), :]).astype(BF16)
            if plane == 0:
                fbuf[rows(at, 32), :] = value
            fill_f(plane, 2 * j + q, value)

    each(4, lambda j: first_back(0, j, mm(bd2[0:128, :], S2[rows(j * 128, 256), :])))

    @pl.when(has_lower)
    def _():
        send_f.start()

    def scatter(G, R, s_sem, r_sem):
        def step(d, carry):
            to = partner(d)
            pltpu.make_async_remote_copy(
                src_ref=G.at[to], dst_ref=R.at[me], send_sem=s_sem.at[d], recv_sem=r_sem.at[me],
                device_id=(group, to), device_id_type=MESH,
            ).start()
            return carry

        lax.fori_loop(1, n, step, 0)
        R[me] = G[me]

    def gather_total(G, R, T, s_sem, r_sem, t_s, t_r):
        def arrive(d, carry):
            other = partner(d)
            pltpu.make_async_remote_copy(
                src_ref=G.at[other], dst_ref=R.at[other], send_sem=s_sem.at[d], recv_sem=r_sem.at[other],
                device_id=(group, other), device_id_type=MESH,
            ).wait()
            return carry

        lax.fori_loop(1, n, arrive, 0)
        T[me] = jnp.sum(R[...], axis=0)

        def step(d, carry):
            pltpu.make_async_remote_copy(
                src_ref=T.at[me], dst_ref=T.at[me], send_sem=t_s.at[d], recv_sem=t_r.at[me],
                device_id=(group, partner(d)), device_id_type=MESH,
            ).start()
            return carry

        lax.fori_loop(1, n, step, 0)

    def collect(T, t_s, t_r):
        def arrive(d, carry):
            other = partner(d)
            pltpu.make_async_remote_copy(
                src_ref=T.at[me], dst_ref=T.at[other], send_sem=t_s.at[d], recv_sem=t_r.at[other],
                device_id=(group, other), device_id_type=MESH,
            ).wait()
            return carry

        lax.fori_loop(1, n, arrive, 0)

    sums = []
    for a in range(3):
        total = jnp.zeros((288, 64), F32)
        for j in range(4):
            total = total + mm_nt(B[a, j * 192:j * 192 + 288, :], S2[j * 128:j * 128 + 64, :])
        sums.append(total * inverse_count)
    packed = jnp.concatenate(
        (
            jnp.concatenate((sums[0], sums[1][0:144, :]), axis=0),
            jnp.concatenate((sums[1][144:288, :], sums[2]), axis=0),
        ),
        axis=1,
    )
    packed = jnp.concatenate((packed, jnp.zeros((n * p2 - 432, 128), F32)), axis=0)
    G2[...] = packed.reshape(n, p2, 128)
    scatter(G2, R2, rs2_s, rs2_r)

    @pl.when(has_upper)
    def _():
        send_s.wait_recv()
        each(4, lambda j: fill_s(SU, j, halo_s[rows(j * 64, 64), :]))

    @pl.when(jnp.logical_not(has_upper))
    def _():
        SU[0:512, :] = jnp.zeros((512, 128), BF16)

    each(4, lambda j: first_back(
        1, j, mm(bd2[128:256, :], S2[rows(j * 128, 256), :]) + mm(bd2[256:384, :], SU[rows(j * 128, 256), :])))

    def first_grad(a):
        def step(j, total):
            for i in range(2):
                total = total + mm_nt(A[2 * i + a, rows(j * 96, 144), :], F2[i, rows(j * 64, 32), :])
            return total

        return lax.fori_loop(0, 8, step, jnp.zeros((144, 32), F32), unroll=True) * inverse_count

    head_column = jnp.concatenate((head, jnp.zeros((80, 1), F32)), axis=0)
    packed = jnp.concatenate(
        [first_grad(a) for a in range(3)] + [jnp.broadcast_to(head_column, (144, 32))], axis=1)
    packed = jnp.concatenate((packed, jnp.zeros((n * p1 - 144, 128), F32)), axis=0)
    G1[...] = packed.reshape(n, p1, 128)
    scatter(G1, R1, rs1_s, rs1_r)

    def put(x, j, value):
        value = value.astype(BF16)
        for q in range(2):
            for z in range(2):
                IGp[x, rows((2 * j + q) * 16, 16), z * 256:(z + 1) * 256] = value[q * 32 + z * 16:q * 32 + z * 16 + 16, :]

    def own_planes(j):
        at = rows(j * 64, 128)
        low = mm(bd1[0:128, :], F2[0, at, :])
        high = mm(bd1[...], F2[1, at, :])
        put(0, j, low[0:64, :])
        put(1, j, low[64:128, :] + high[128:192, :])
        put(2, j, high[0:64, :])

    each(8, own_planes)
    gather_total(G2, R2, T2, rs2_s, rs2_r, ag2_s, ag2_r)
    for x in range(3):
        out[x] = mm(IGp[x], gather[...]).astype(BF16)
    gather_total(G1, R1, T1, rs1_s, rs1_r, ag1_s, ag1_r)

    @pl.when(has_upper)
    def _():
        send_f.wait_recv()
        each(8, lambda j: fill_f(2, j, halo_f[rows(j * 32, 32), :]))

    @pl.when(jnp.logical_not(has_upper))
    def _():
        F2[2, 0:512, :] = jnp.zeros((512, 256), BF16)

    def last_plane(j):
        at = rows(j * 64, 128)
        put(3, j, mm(bd1[64:128, :], F2[1, at, :]) + mm(bd1[128:192, :], F2[2, at, :]))

    each(8, last_plane)
    out[3] = mm(IGp[3], gather[...]).astype(BF16)

    collect(T2, ag2_s, ag2_r)
    second = T2[...].reshape(n * p2, 128)
    sg_out[0:432, :] = second[0:432, 0:64]
    sg_out[432:864, :] = second[0:432, 64:128]
    collect(T1, ag1_s, ag1_r)
    first = T1[...].reshape(n * p1, 128)
    for a in range(3):
        fg_out[a * 144:(a + 1) * 144, :] = first[0:144, a * 32:(a + 1) * 32]
    head_out[...] = jnp.sum(jnp.where(diagonal, first[0:64, 96:97], 0.0), axis=0, keepdims=True)

    @pl.when(has_upper)
    def _():
        send_a.wait_send()
        send_b.wait_send()

    @pl.when(has_lower)
    def _():
        send_s.wait_send()
        send_f.wait_send()


def shards(n, activations, first_kernel, second_kernel, head_weight, labels):
    inverse_count = 1.0 / (labels.size * n)
    p1 = 8 * -(-144 // (8 * n))
    p2 = 8 * -(-432 // (8 * n))
    vmem = pl.BlockSpec(memory_space=pltpu.VMEM)
    dma = pltpu.SemaphoreType.DMA
    out, first, second, head = pl.pallas_call(
        functools.partial(kernel, n, p1, p2, inverse_count),
        out_shape=(
            jax.ShapeDtypeStruct((4, 256, 512), BF16),
            jax.ShapeDtypeStruct((432, 32), F32),
            jax.ShapeDtypeStruct((864, 64), F32),
            jax.ShapeDtypeStruct((1, 64), F32),
        ),
        in_specs=[vmem] * 5,
        out_specs=(vmem,) * 4,
        scratch_shapes=[
            pltpu.VMEM((5, 816, 256), BF16),
            pltpu.VMEM((3, 864, 128), BF16),
            pltpu.VMEM((640, 128), BF16),
            pltpu.VMEM((640, 128), BF16),
            pltpu.VMEM((3, 576, 256), BF16),
            pltpu.VMEM((2, 256, 256), F32),
            pltpu.VMEM((4, 256, 512), BF16),
            pltpu.VMEM((512, 640), BF16),
            pltpu.VMEM((512, 512), BF16),
            pltpu.VMEM((3, 32, 144), BF16),
            pltpu.VMEM((3, 64, 288), BF16),
            pltpu.VMEM((192, 128), BF16),
            pltpu.VMEM((384, 256), BF16),
            pltpu.VMEM((256, 256), BF16),
            pltpu.VMEM((256, 128), BF16),
            pltpu.VMEM((256, 256), BF16),
            pltpu.VMEM((256, 512), BF16),
            pltpu.VMEM((256, 256), BF16),
            pltpu.VMEM((256, 128), BF16),
            pltpu.VMEM((256, 256), BF16),
        ]
        + [pltpu.VMEM((n, p1, 128), F32)] * 3
        + [pltpu.VMEM((n, p2, 128), F32)] * 3
        + [dma((4,)), dma((4,))]
        + [dma((n,))] * 8,
        compiler_params=pltpu.CompilerParams(
            collective_id=0, has_side_effects=True, vmem_limit_bytes=40 * 1024 * 1024
        ),
    )(
        activations.reshape(4, 256, 512),
        first_kernel.reshape(432, 32),
        second_kernel.reshape(864, 64),
        head_weight.reshape(1, 64),
        labels,
    )
    return (
        out.reshape(activations.shape),
        first.reshape(first_kernel.shape),
        second.reshape(second_kernel.shape),
        head.reshape(head_weight.shape),
    )


def solution(mesh):
    return jax.shard_map(
        functools.partial(shards, mesh.shape["gx"]),
        mesh=mesh,
        in_specs=(
            P(("groups", "gx"), None, None, None),
            P(),
            P(),
            P(),
            P(("groups", "gx"), None, None),
        ),
        out_specs=(
            P(("groups", "gx"), None, None, None),
            P("groups", None, None, None, None),
            P("groups", None, None, None, None),
            P("groups"),
        ),
        check_vma=False,
    )
```

```python
import functools

import jax
import jax.numpy as jnp
from jax import lax
from jax.experimental import pallas as pl
from jax.experimental.pallas import tpu as pltpu
from jax.sharding import PartitionSpec as P

F32 = jnp.float32
BF16 = jnp.bfloat16
MESH = pl.DeviceIdType.MESH


def mm(left, right):
    return lax.dot_general(left, right, (((1,), (0,)), ((), ())), preferred_element_type=F32)


def mm_nt(left, right):
    return lax.dot_general(left, right, (((1,), (1,)), ((), ())), preferred_element_type=F32)


def iota(shape, axis):
    return lax.broadcasted_iota(jnp.int32, shape, axis)


def one_hot(condition):
    return jnp.where(condition, 1.0, 0.0).astype(BF16)


def each(count, body):
    def step(index, carry):
        body(index)
        return carry

    lax.fori_loop(0, count, step, 0, unroll=True)


def rows(start, size, align=16):
    return pl.ds(pl.multiple_of(start, align), size)


def roll_masked(value, shift, empty_lane):
    rolled = pltpu.roll(value, shift, axis=1)
    return jnp.where(iota(value.shape, 1) == empty_lane, 0.0, rolled)


def kernel(
    n, inverse_count,
    act_hbm, w1_hbm, w2_hbm, hw_hbm, labels_hbm,
    out_hbm, fg_out, sg_out, head_out,
    A, B, S2, SU, F2, slope1, IGp, spread, gather, w1t, w2t, bd1, bd2,
    abuf, sbuf, fbuf, halo_a, halo_b, halo_s, halo_f,
    G1, R1, T1, G2, R2, T2,
    act, w1, w2, hw, labels, load, out,
    halo_send, halo_recv, rs1_s, rs1_r, ag1_s, ag1_r, rs2_s, rs2_r, ag2_s, ag2_r,
):
    me = lax.axis_index("gx")
    group = lax.axis_index("groups")
    has_lower = me > 0
    has_upper = me < n - 1

    def partner(d):
        return lax.rem(me + d, n)

    barrier = pltpu.get_barrier_semaphore()

    def greet(d, carry):
        pl.semaphore_signal(barrier, inc=1, device_id=(group, partner(d)), device_id_type=MESH)
        return carry

    lax.fori_loop(1, n, greet, 0)

    loads = [pltpu.make_async_copy(act_hbm.at[x], act.at[x], load.at[x]) for x in range(4)]
    smalls = [
        pltpu.make_async_copy(source, target, load.at[4 + k])
        for k, (source, target) in enumerate(((w1_hbm, w1), (w2_hbm, w2), (hw_hbm, hw), (labels_hbm, labels)))
    ]
    for copy in smalls + [loads[x] for x in (1, 2, 3, 0)]:
        copy.start()

    z_row = iota((512, 640), 0)
    lane = iota((512, 640), 1)
    spread[...] = one_hot(z_row == 4 * (lane & 127) + (lane >> 7) - 1)
    src = iota((512, 512), 0)
    gather[...] = one_hot(iota((512, 512), 1) == 4 * (src & 127) + 2 * ((src >> 7) & 1) + (src >> 8))

    pl.semaphore_wait(barrier, n - 1)

    def halo(slot, source, target, to):
        return pltpu.make_async_remote_copy(
            src_ref=source, dst_ref=target, send_sem=halo_send.at[slot], recv_sem=halo_recv.at[slot],
            device_id=(group, to), device_id_type=MESH,
        )

    up = lax.rem(me + 1, n)
    down = lax.rem(me + n - 1, n)
    send_a = halo(0, act_hbm.at[3], halo_a, up)
    send_b = halo(1, abuf, halo_b, up)
    send_s = halo(2, sbuf, halo_s, down)
    send_f = halo(3, fbuf, halo_f, down)

    @pl.when(has_upper)
    def _():
        send_a.start()

    for copy in smalls:
        copy.wait()

    eye32 = one_hot(iota((32, 32), 0) == iota((32, 32), 1))
    eye64 = one_hot(iota((64, 64), 0) == iota((64, 64), 1))
    for a in range(3):
        w1t[a] = mm_nt(eye32, w1[a * 144:(a + 1) * 144, :]).astype(BF16)
        w2t[a] = mm_nt(eye64, w2[a * 288:(a + 1) * 288, :]).astype(BF16)
    for place, a in enumerate((1, 2, 0)):
        def k1(b, c):
            at = (a * 9 + b * 3 + c) * 16
            return w1[at:at + 16, :].astype(F32)

        def k2(b, c):
            at = (a * 9 + b * 3 + c) * 32
            return w2[at:at + 32, :].astype(F32)

        zero1 = jnp.zeros((16, 32), F32)
        zero2 = jnp.zeros((32, 64), F32)
        for k, zero, dest, height in ((k1, zero1, bd1, 16), (k2, zero2, bd2, 32)):
            table = (
                (k(1, 1), zero, zero, zero),
                (k(1, 2), k(1, 0), zero, zero),
                (k(2, 1), zero, k(0, 1), zero),
                (k(2, 2), k(2, 0), k(0, 2), k(0, 0)),
            )
            for q, parts in enumerate(table):
                at = place * 4 * height + q * height
                dest[at:at + height, :] = jnp.concatenate(parts, axis=1).astype(BF16)

    for x in range(5):
        A[x, 0:48, :] = jnp.zeros((48, 256), BF16)
    for x in range(3):
        B[x, 0:96, :] = jnp.zeros((96, 128), BF16)
        F2[x, 512:576, :] = jnp.zeros((64, 256), BF16)
    S2[512:640, :] = jnp.zeros((128, 128), BF16)
    SU[512:640, :] = jnp.zeros((128, 128), BF16)

    def fill_a(x, plane):
        phases = mm(plane, spread[...]).astype(BF16)
        for y in range(16):
            part = phases[y * 16:(y + 1) * 16, :]
            for c in range(3):
                at = (y + 1) * 48 + c * 16
                A[x, at:at + 16, 0:128] = part[:, c * 128:(c + 1) * 128]
                A[x, at:at + 16, 128:256] = part[:, (c + 2) * 128:(c + 3) * 128]

    def fill_b(x, j, value):
        even = value[:, 0:128]
        odd = value[:, 128:256]
        back = roll_masked(odd.astype(F32), 1, 0).astype(BF16)
        at = (j + 1) * 96
        B[x, rows(at, 32), :] = back
        B[x, rows(at + 32, 32), :] = even
        B[x, rows(at + 64, 32), :] = odd

    def first_section(i):
        def body(j):
            at = rows(j * 96, 144)
            pre = mm(w1t[0], A[2 * i, at, :]) + mm(w1t[1], A[2 * i + 1, at, :]) + mm(w1t[2], A[2 * i + 2, at, :])
            sig = jax.nn.sigmoid(pre)
            slope1[i, rows(j * 32, 32), :] = sig * (1.0 + pre * (1.0 - sig))
            value = (pre * sig).astype(BF16)
            if i == 1:
                abuf[rows(j * 32, 32), :] = value
            fill_b(i + 1, j, value)

        each(8, body)

    for x in (1, 2, 3):
        loads[x].wait()
        fill_a(x + 1, act[x])
    first_section(1)

    @pl.when(has_upper)
    def _():
        send_b.start()

    loads[0].wait()
    fill_a(1, act[0])

    @pl.when(has_lower)
    def _():
        send_a.wait_recv()
        fill_a(0, halo_a[...])

    @pl.when(jnp.logical_not(has_lower))
    def _():
        A[0] = jnp.zeros((816, 256), BF16)

    first_section(0)

    @pl.when(has_lower)
    def _():
        send_b.wait_recv()
        each(8, lambda j: fill_b(0, j, halo_b[rows(j * 32, 32), :]))

    @pl.when(jnp.logical_not(has_lower))
    def _():
        B[0] = jnp.zeros((864, 128), BF16)

    diagonal = iota((64, 64), 0) == iota((64, 64), 1)
    weight = jnp.sum(jnp.where(diagonal, hw[...], 0.0), axis=1, keepdims=True)

    def fill_s(target, j, value):
        at = j * 128
        target[rows(at, 64), :] = value
        target[rows(at + 64, 64), :] = roll_masked(value.astype(F32), 127, 127).astype(BF16)

    head = jnp.zeros((64, 128), F32)
    for j in range(4):
        at = slice(j * 192, j * 192 + 288)
        pre = mm(w2t[0], B[0, at, :]) + mm(w2t[1], B[1, at, :]) + mm(w2t[2], B[2, at, :])
        sig = jax.nn.sigmoid(pre)
        act2 = pre * sig
        logits = jnp.sum(act2 * weight, axis=0, keepdims=True)
        logit_grad = jax.nn.sigmoid(logits) - labels[0, j:j + 1, :].astype(F32)
        head = head + logit_grad * act2
        slope = (logit_grad * weight * (sig * (1.0 + pre * (1.0 - sig)))).astype(BF16)
        sbuf[j * 64:(j + 1) * 64, :] = slope
        fill_s(S2, j, slope)
    head = jnp.sum(head, axis=1, keepdims=True) * inverse_count

    @pl.when(has_lower)
    def _():
        send_s.start()

    def fill_f(plane, j, value):
        even = value[:, 0:128]
        ahead = roll_masked(even.astype(F32), 127, 127).astype(BF16)
        at = j * 64
        F2[plane, rows(at, 32), :] = value
        F2[plane, rows(at + 32, 32), 0:128] = value[:, 128:256]
        F2[plane, rows(at + 32, 32), 128:256] = ahead

    def first_back(plane, j, back):
        for q in range(2):
            at = (2 * j + q) * 32
            both = jnp.concatenate((back[q * 64:q * 64 + 32, :], back[q * 64 + 32:q * 64 + 64, :]), axis=1)
            value = (both * slope1[plane, rows(at, 32), :]).astype(BF16)
            if plane == 0:
                fbuf[rows(at, 32), :] = value
            fill_f(plane, 2 * j + q, value)

    each(4, lambda j: first_back(0, j, mm(bd2[0:128, :], S2[rows(j * 128, 256), :])))

    @pl.when(has_lower)
    def _():
        send_f.start()

    def base(G):
        return (n - G.shape[0]) // 2

    def owns(G, device):
        return jnp.logical_and(device >= base(G), device < base(G) + G.shape[0])

    def scatter(G, R, s_sem, r_sem):
        def step(d, carry):
            to = partner(d)

            @pl.when(owns(G, to))
            def _():
                q = to - base(G)
                pltpu.make_async_remote_copy(
                    src_ref=G.at[q], dst_ref=R.at[me], send_sem=s_sem.at[q], recv_sem=r_sem.at[me],
                    device_id=(group, to), device_id_type=MESH,
                ).start()

            return carry

        lax.fori_loop(1, n, step, 0, unroll=n <= 16)

    def gather_total(G, R, T, s_sem, r_sem, t_s, t_r, split):
        @pl.when(owns(G, me))
        def _():
            q = me - base(G)
            R[me] = G[q]

            def arrive(d, carry):
                other = partner(d)
                pltpu.make_async_remote_copy(
                    src_ref=G.at[q], dst_ref=R.at[other], send_sem=s_sem.at[q], recv_sem=r_sem.at[other],
                    device_id=(group, other), device_id_type=MESH,
                ).wait_recv()
                return carry

            lax.fori_loop(1, n, arrive, 0)
            total = jnp.sum(R[...].astype(F32), axis=0)
            if split:
                total = join(total)
            T[q] = total.astype(BF16) if not split else halves(total)

            def step(d, carry):
                to = partner(d)
                pltpu.make_async_remote_copy(
                    src_ref=T.at[q], dst_ref=T.at[q], send_sem=t_s.at[to], recv_sem=t_r.at[q],
                    device_id=(group, to), device_id_type=MESH,
                ).start()
                return carry

            lax.fori_loop(1, n, step, 0, unroll=n <= 16)

    def collect(T, t_s, t_r):
        def arrive(q, carry):
            source = q + base(T)

            @pl.when(source != me)
            def _():
                pltpu.make_async_remote_copy(
                    src_ref=T.at[q], dst_ref=T.at[q], send_sem=t_s.at[source], recv_sem=t_r.at[q],
                    device_id=(group, source), device_id_type=MESH,
                ).wait_recv()

            return carry

        lax.fori_loop(0, T.shape[0], arrive, 0)

    def drain(G, R, T, s_sem, r_sem, t_s, t_r):
        def sent(q, carry):
            to = q + base(G)

            @pl.when(to != me)
            def _():
                pltpu.make_async_remote_copy(
                    src_ref=G.at[q], dst_ref=R.at[me], send_sem=s_sem.at[q], recv_sem=r_sem.at[me],
                    device_id=(group, to), device_id_type=MESH,
                ).wait_send()

            return carry

        lax.fori_loop(0, G.shape[0], sent, 0)

        @pl.when(owns(G, me))
        def _():
            q = me - base(G)

            def step(d, carry):
                to = partner(d)
                pltpu.make_async_remote_copy(
                    src_ref=T.at[q], dst_ref=T.at[q], send_sem=t_s.at[to], recv_sem=t_r.at[q],
                    device_id=(group, to), device_id_type=MESH,
                ).wait_send()
                return carry

            lax.fori_loop(1, n, step, 0)

    def join(value):
        return value + jnp.where(iota(value.shape, 1) == 96, pltpu.roll(value, 127, axis=1), 0.0)

    def halves(value):
        rounded = value.astype(BF16).astype(F32)
        rest = pltpu.roll(value - rounded, 1, axis=1)
        return jnp.where(iota(value.shape, 1) == 97, rest, rounded).astype(BF16)

    def pack(value, G):
        flat = G.shape[0] * G.shape[1]
        if flat > value.shape[0]:
            value = jnp.concatenate((value, jnp.zeros((flat - value.shape[0], 128), BF16)), axis=0)
        G[...] = value.reshape(G.shape)

    sums = []
    for a in range(3):
        total = jnp.zeros((288, 64), F32)
        for j in range(4):
            total = total + mm_nt(B[a, j * 192:j * 192 + 288, :], S2[j * 128:j * 128 + 64, :])
        sums.append(total * inverse_count)
    packed = jnp.concatenate(
        (
            jnp.concatenate((sums[0], sums[1][0:144, :]), axis=0),
            jnp.concatenate((sums[1][144:288, :], sums[2]), axis=0),
        ),
        axis=1,
    )
    pack(packed.astype(BF16), G2)
    scatter(G2, R2, rs2_s, rs2_r)

    @pl.when(has_upper)
    def _():
        send_s.wait_recv()
        each(4, lambda j: fill_s(SU, j, halo_s[rows(j * 64, 64), :]))

    @pl.when(jnp.logical_not(has_upper))
    def _():
        SU[0:512, :] = jnp.zeros((512, 128), BF16)

    each(4, lambda j: first_back(
        1, j, mm(bd2[128:256, :], S2[rows(j * 128, 256), :]) + mm(bd2[256:384, :], SU[rows(j * 128, 256), :])))

    def first_grad(a):
        def step(j, total):
            for i in range(2):
                total = total + mm_nt(A[2 * i + a, rows(j * 96, 144), :], F2[i, rows(j * 64, 32), :])
            return total

        return lax.fori_loop(0, 8, step, jnp.zeros((144, 32), F32), unroll=True) * inverse_count

    head_column = jnp.concatenate((head, jnp.zeros((80, 1), F32)), axis=0)
    packed = jnp.concatenate(
        [first_grad(a) for a in range(3)] + [jnp.broadcast_to(head_column, (144, 32))], axis=1)
    pack(halves(packed), G1)
    scatter(G1, R1, rs1_s, rs1_r)

    stores = [pltpu.make_async_copy(out.at[x], out_hbm.at[x], load.at[x]) for x in range(4)]

    def store(x):
        out[x] = mm(IGp[x], gather[...]).astype(BF16)
        stores[x].start()

    def put(x, j, value):
        value = value.astype(BF16)
        for q in range(2):
            for z in range(2):
                IGp[x, rows((2 * j + q) * 16, 16), z * 256:(z + 1) * 256] = value[q * 32 + z * 16:q * 32 + z * 16 + 16, :]

    def own_planes(j):
        at = rows(j * 64, 128)
        low = mm(bd1[0:128, :], F2[0, at, :])
        high = mm(bd1[...], F2[1, at, :])
        put(0, j, low[0:64, :])
        put(1, j, low[64:128, :] + high[128:192, :])
        put(2, j, high[0:64, :])

    each(8, own_planes)
    gather_total(G2, R2, T2, rs2_s, rs2_r, ag2_s, ag2_r, False)
    for x in range(3):
        store(x)
    gather_total(G1, R1, T1, rs1_s, rs1_r, ag1_s, ag1_r, True)

    @pl.when(has_upper)
    def _():
        send_f.wait_recv()
        each(8, lambda j: fill_f(2, j, halo_f[rows(j * 32, 32), :]))

    @pl.when(jnp.logical_not(has_upper))
    def _():
        F2[2, 0:512, :] = jnp.zeros((512, 256), BF16)

    def last_plane(j):
        at = rows(j * 64, 128)
        put(3, j, mm(bd1[64:128, :], F2[1, at, :]) + mm(bd1[128:192, :], F2[2, at, :]))

    each(8, last_plane)
    store(3)

    collect(T2, ag2_s, ag2_r)
    second = T2[...].astype(F32).reshape(-1, 128)
    sg_out[0:432, :] = second[0:432, 0:64]
    sg_out[432:864, :] = second[0:432, 64:128]
    collect(T1, ag1_s, ag1_r)
    first = T1[...].astype(F32).reshape(-1, 128)
    for a in range(3):
        fg_out[a * 144:(a + 1) * 144, :] = first[0:144, a * 32:(a + 1) * 32]
    head_out[...] = jnp.sum(jnp.where(diagonal, join(first)[0:64, 96:97], 0.0), axis=0, keepdims=True)

    @pl.when(has_upper)
    def _():
        send_a.wait_send()
        send_b.wait_send()

    @pl.when(has_lower)
    def _():
        send_s.wait_send()
        send_f.wait_send()

    for copy in stores:
        copy.wait()
    drain(G2, R2, T2, rs2_s, rs2_r, ag2_s, ag2_r)
    drain(G1, R1, T1, rs1_s, rs1_r, ag1_s, ag1_r)


def cut(units, n):
    size = -(-units // n)
    return -(-units // size), 16 * size


def shards(n, activations, first_kernel, second_kernel, head_weight, labels):
    inverse_count = 1.0 / (labels.size * n)
    q1, p1 = cut(9, n)
    q2, p2 = cut(27, n)
    vmem = pl.BlockSpec(memory_space=pltpu.VMEM)
    dma = pltpu.SemaphoreType.DMA
    hbm = pl.BlockSpec(memory_space=pltpu.HBM)
    results = (
        jax.ShapeDtypeStruct((4, 256, 512), BF16),
        jax.ShapeDtypeStruct((432, 32), F32),
        jax.ShapeDtypeStruct((864, 64), F32),
        jax.ShapeDtypeStruct((1, 64), F32),
    )
    out, first, second, head = pl.pallas_call(
        functools.partial(kernel, n, inverse_count),
        out_shape=results,
        in_specs=[hbm] * 5,
        out_specs=(hbm, vmem, vmem, vmem),
        scratch_shapes=[
            pltpu.VMEM((5, 816, 256), BF16),
            pltpu.VMEM((3, 864, 128), BF16),
            pltpu.VMEM((640, 128), BF16),
            pltpu.VMEM((640, 128), BF16),
            pltpu.VMEM((3, 576, 256), BF16),
            pltpu.VMEM((2, 256, 256), F32),
            pltpu.VMEM((4, 256, 512), BF16),
            pltpu.VMEM((512, 640), BF16),
            pltpu.VMEM((512, 512), BF16),
            pltpu.VMEM((3, 32, 144), BF16),
            pltpu.VMEM((3, 64, 288), BF16),
            pltpu.VMEM((192, 128), BF16),
            pltpu.VMEM((384, 256), BF16),
            pltpu.VMEM((256, 256), BF16),
            pltpu.VMEM((256, 128), BF16),
            pltpu.VMEM((256, 256), BF16),
            pltpu.VMEM((256, 512), BF16),
            pltpu.VMEM((256, 256), BF16),
            pltpu.VMEM((256, 128), BF16),
            pltpu.VMEM((256, 256), BF16),
        ]
        + [pltpu.VMEM((pieces, p1, 128), BF16) for pieces in (q1, n, q1)]
        + [pltpu.VMEM((pieces, p2, 128), BF16) for pieces in (q2, n, q2)]
        + [
            pltpu.VMEM((4, 256, 512), BF16),
            pltpu.VMEM((432, 32), BF16),
            pltpu.VMEM((864, 64), BF16),
            pltpu.VMEM((1, 64), F32),
            pltpu.VMEM(labels.shape, labels.dtype),
            dma((8,)),
            pltpu.VMEM((4, 256, 512), BF16),
        ]
        + [dma((4,)), dma((4,))]
        + [dma((q1,)), dma((n,)), dma((n,)), dma((q1,))]
        + [dma((q2,)), dma((n,)), dma((n,)), dma((q2,))],
        compiler_params=pltpu.CompilerParams(
            collective_id=0, has_side_effects=True, vmem_limit_bytes=63 * 1024 * 1024
        ),
    )(
        activations.reshape(4, 256, 512),
        first_kernel.reshape(432, 32),
        second_kernel.reshape(864, 64),
        head_weight.reshape(1, 64),
        labels,
    )
    return (
        out.reshape(activations.shape),
        first.reshape(first_kernel.shape),
        second.reshape(second_kernel.shape),
        head.reshape(head_weight.shape),
    )


def solution(mesh):
    return jax.shard_map(
        functools.partial(shards, mesh.shape["gx"]),
        mesh=mesh,
        in_specs=(
            P(("groups", "gx"), None, None, None),
            P(),
            P(),
            P(),
            P(("groups", "gx"), None, None),
        ),
        out_specs=(
            P(("groups", "gx"), None, None, None),
            P("groups", None, None, None, None),
            P("groups", None, None, None, None),
            P("groups"),
        ),
        check_vma=False,
    )
```
